32 devices in a mesh: ka: 8 (over z, x), pts: 4 (over y, core).
Axes of the slice: x: 2, y: 2, z: 4, core: 2. Of those that a mesh axis runs over, the one named last changes fastest.
Arguments:
- valence: bfloat16 [8, 32, 4096], P('ka', None, 'pts'), may hold values from -0.09375 to 0.09375
- conduction: bfloat16 [8, 32, 4096], P('ka', None, 'pts'), may hold values from -6 to 6
- trials: bfloat16 [8, 32, 256], P('ka'), may hold values from -6 to 6
- w_panels: bfloat16 [8, 4096, 4096], P('ka', 'pts'), may hold values from -0.109375 to 0.109375
- partner: int32 [3, 8], replicated, may hold values from 0 to 7, as said below
- owner: int32 [3], replicated, may hold values from 0 to 7, as said below
Outputs:
- applied: float32 [8, 32, 256], P('ka', None, 'pts')
The draws below stay inside these ranges and needn't reach their ends.
Inputs may be any that keep to these rules, and one draw needn't show every extreme that they name: For each q there is a displacement d with partner[q, k] = (k + d) mod 8 for every k; the 3 displacements differ, are not 0, and include 8 - 1 and 4. `owner`: the 3 entries differ.
All inputs are finite; a program needn't handle non-finite values.
Results may differ from the reference program's by a relative error of at most 0.005.
Values may be sent and summed in bfloat16 or wider, within the bound.
A program may use at most 64 MiB of HBM per device.

```python
import math
import jax
import jax.numpy as jnp
from jax import lax

NV = 32
NC = 32
NMU = 4096
NQ = 3
TR = 8
K = 8


def draw_partner(key, part):
    pick = jax.random.randint(jax.random.fold_in(key, 11), (), 0, K - 3).astype(jnp.int32) + 1
    pick = pick + (pick >= K // 2).astype(jnp.int32)
    fixed_set = jnp.stack([pick, jnp.int32(K // 2), jnp.int32(K - 1)]).astype(jnp.int32)
    order = jax.random.permutation(jax.random.fold_in(key, 13), 3)
    offsets = fixed_set[order][:NQ]
    return ((jnp.arange(K, dtype=jnp.int32)[None, :] + offsets[:, None].astype(jnp.int32)) % K).astype(jnp.int32)


def draw_owner(key, part):
    middle = jax.random.randint(jax.random.fold_in(key, 23), (), 1, K - 1).astype(jnp.int32)
    slots = jnp.stack([jnp.int32(0), middle, jnp.int32(K - 1)]).astype(jnp.int32)
    order = jax.random.permutation(jax.random.fold_in(key, 29), 3)
    return slots[order][:NQ].astype(jnp.int32)


def shard_levels(own_key, shape, cuts, least, largest):
    def one(position, shards_of):
        heights = jax.random.uniform(jax.random.fold_in(jax.random.fold_in(own_key, 6), position), (shards_of,), jnp.float32, least / len(cuts), largest / len(cuts))
        return jnp.repeat(jnp.exp(heights), shape[position] // shards_of).reshape((-1,) + (1,) * (len(shape) - position - 1))

    factor_of = one(*cuts[0])
    for cut in cuts[1:]:
        factor_of = factor_of * one(*cut)
    return factor_of


def scatter_about(key, shape, scale, bound, pieces=(), kind=jnp.bfloat16):
    array = jax.random.normal(key, shape, jnp.float32) * scale
    if len(pieces) > 0:
        array = shard_levels(key, shape, pieces, -0.22, 0.18) * array
    return jnp.clip(array, min=-bound, max=bound).astype(kind)


def setup_inputs(seed: int = 0) -> dict:
    streams_of = jax.random.split(jax.random.key(seed), 7)
    return {
        "valence": scatter_about(streams_of[0], (K, NV, NMU), NMU ** -0.5, 0.09375, ((0, 8), (2, 4))),
        "conduction": scatter_about(streams_of[1], (K, NC, NMU), 1.0, 6.0, ((0, 8), (2, 4))),
        "trials": scatter_about(streams_of[2], (K, NV, NC * TR), 1.0, 6.0, ((0, 8),)),
        "w_panels": scatter_about(streams_of[3], (K, NMU, NMU), (3 * NV * NC) ** -0.5, 0.109375, ((0, 8), (1, 4))),
        "partner": draw_partner(jax.random.fold_in(streams_of[6], 71), 0),
        "owner": draw_owner(jax.random.fold_in(streams_of[6], 71), 0),
    }


def reference(valence, conduction, trials, w_panels, partner, owner):
    width = math.gcd(NMU, 512)
    nblocks = NMU // width

    def one_point(kidx):
        total = jnp.zeros((NV, NC, TR), jnp.float32)
        own_val = valence[kidx].astype(jnp.float32)
        own_cond = conduction[kidx].reshape(NC, nblocks, width).transpose(1, 0, 2)
        for q in range(NQ):
            other = partner[q, kidx]
            panel = w_panels[owner[q]].reshape(nblocks, width, NMU)
            far_val = valence[other].astype(jnp.float32)
            far_cond = conduction[other].astype(jnp.float32)
            far_trial = trials[other].reshape(NV, NC, TR).astype(jnp.float32)
            block = jnp.einsum("cm,vct->mvt", far_cond, far_trial).astype(jnp.bfloat16)
            block = block.reshape(nblocks, width, NV, TR)

            def one_block(items):
                piece, rows, cond_rows = items
                image = jnp.einsum("mvt,vn->mnt", piece.astype(jnp.float32), far_val)
                weighted = (rows.astype(jnp.float32)[:, :, None] * image).astype(jnp.bfloat16)
                back = jnp.einsum("mnt,wn->mwt", weighted.astype(jnp.float32), own_val)
                return jnp.einsum("cm,mwt->wct", cond_rows.astype(jnp.float32), back)

            total = total + jnp.sum(lax.map(one_block, (block, panel, own_cond)), axis=0)
        return total.reshape(NV, NC * TR)

    return lax.map(one_point, jnp.arange(K, dtype=jnp.int32))
```

```python
import functools

import jax
import jax.numpy as jnp
from jax import lax
from jax.experimental import pallas as pl
from jax.experimental.pallas import tpu as pltpu
from jax.sharding import PartitionSpec as P

NT = (((1,), (1,)), ((), ()))


def dot_nt(a, b):
    return lax.dot_general(a, b, NT, preferred_element_type=jnp.float32)


def panel_kernel(
    active, partner, w_ref, val_ref, cond_ref, trial_ref, out_ref, pair_ref, z_ref, block_ref, back_ref,
    *, nk, npart, bands, ntrial, rows,
):
    width = val_ref.shape[2]
    points = w_ref.shape[0]
    out_ref[...] = jnp.zeros_like(out_ref)

    def one_k(k, carry):
        p = partner[k]
        block_ref[...] = (
            jnp.dot(trial_ref[p], cond_ref[p], preferred_element_type=jnp.float32)
            .astype(jnp.bfloat16)
            .astype(jnp.float32)
        )

        def pairs(j, c):
            own = val_ref[k * npart + j]
            far = val_ref[p * npart + j]
            cols = pl.ds(pl.multiple_of(j * width, width), width)
            for v in range(bands):
                pair_ref[v * bands : (v + 1) * bands, cols] = own * far[v : v + 1, :]
            return c

        lax.fori_loop(0, npart, pairs, 0)

        def some_rows(b, c):
            here = pl.ds(pl.multiple_of(b * rows, rows), rows)
            z_ref[...] = dot_nt(pair_ref[...], w_ref[here, :])

            def lanes(l, cc):
                off = pl.multiple_of(l * 128, 128)
                mine = pl.ds(pl.multiple_of(b * rows + off, 128), 128)
                acc = [jnp.zeros((bands, 128), jnp.float32) for _ in range(ntrial)]
                for v in range(bands):
                    z = z_ref[v * bands : (v + 1) * bands, pl.ds(off, 128)]
                    for t in range(ntrial):
                        acc[t] = acc[t] + z * block_ref[pl.ds(t * bands + v, 1), mine]
                for t in range(ntrial):
                    back_ref[t * bands : (t + 1) * bands, pl.ds(off, 128)] = acc[t]
                return cc

            lax.fori_loop(0, rows // 128, lanes, 0)
            back = back_ref[...]
            high = back.astype(jnp.bfloat16)
            low = (back - high.astype(jnp.float32)).astype(jnp.bfloat16)
            cond = cond_ref[k, :, here]
            out_ref[k] += dot_nt(cond, high) + dot_nt(cond, low)
            return c

        return lax.fori_loop(0, points // rows, some_rows, carry)

    lax.fori_loop(0, nk * active[0], one_k, 0)


def panel_term(active, partner, w, val, cond, trial, npart, ntrial):
    nk, conds, _ = cond.shape
    bands = val.shape[1]
    points, total = w.shape
    rows = min(256, points)
    vm = pl.BlockSpec(memory_space=pltpu.VMEM)
    sm = pl.BlockSpec(memory_space=pltpu.SMEM)
    return pl.pallas_call(
        functools.partial(
            panel_kernel, nk=nk, npart=npart, bands=bands, ntrial=ntrial, rows=rows
        ),
        out_shape=jax.ShapeDtypeStruct((nk, conds, ntrial * bands), jnp.float32),
        in_specs=[sm, sm, vm, vm, vm, vm],
        out_specs=vm,
        scratch_shapes=[
            pltpu.VMEM((bands * bands, total), jnp.bfloat16),
            pltpu.VMEM((bands * bands, rows), jnp.float32),
            pltpu.VMEM((ntrial * bands, points), jnp.float32),
            pltpu.VMEM((ntrial * bands, rows), jnp.float32),
        ],
        compiler_params=pltpu.CompilerParams(vmem_limit_bytes=48 * 1024 * 1024),
    )(active, partner, w, val, cond, trial)


def shards(valence, conduction, trials, w_panels, partner, owner):
    nk = lax.axis_size("ka")
    npart = lax.axis_size("pts")
    me = lax.axis_index("ka")
    bands = valence.shape[1]
    conds = conduction.shape[1]
    width = valence.shape[2]
    ntrial = trials.shape[2] // conds
    val = lax.all_gather(valence[0], ("ka", "pts"), axis=0)
    turned = trials.reshape(1, bands, conds, ntrial).transpose(0, 3, 1, 2)
    turned = turned.reshape(1, ntrial * bands, conds)
    cond = lax.all_gather(conduction, "ka", axis=0, tiled=True)
    trial = lax.all_gather(turned, "ka", axis=0, tiled=True)
    hit = owner == me
    active = jnp.any(hit).astype(jnp.int32).reshape(1)
    mine = jnp.sum(jnp.where(hit[:, None], partner, 0), axis=0).astype(jnp.int32)
    part = panel_term(active, mine, w_panels[0], val, cond, trial, npart, ntrial)
    share = conds // npart
    part = part.reshape(nk * npart, share, ntrial * bands)
    total = lax.psum_scatter(part, ("ka", "pts"), scatter_dimension=0, tiled=True)
    return (
        total.reshape(share, ntrial, bands).transpose(2, 0, 1).reshape(1, bands, share * ntrial)
    )


def solution(mesh):
    placed = (
        P("ka", None, "pts"),
        P("ka", None, "pts"),
        P("ka", None, None),
        P("ka", "pts", None),
        P(),
        P(),
    )
    return jax.shard_map(
        shards, mesh=mesh, in_specs=placed, out_specs=P("ka", None, "pts"), check_vma=False
    )
```

```python
import functools

import jax
import jax.numpy as jnp
from jax import lax
from jax.experimental import pallas as pl
from jax.experimental.pallas import tpu as pltpu
from jax.sharding import PartitionSpec as P

NT = (((1,), (1,)), ((), ()))
TN = (((0,), (0,)), ((), ()))


def dot_nt(a, b):
    return lax.dot_general(a, b, NT, preferred_element_type=jnp.float32)


def gather_kernel(
    nk, npart, v_ref, c_ref, t_ref, val_ref, cond_ref, trial_ref,
    far_send, far_recv, near_send, near_recv, own_sem,
):
    k = lax.axis_index("ka")
    j = lax.axis_index("pts")
    mesh_id = pl.DeviceIdType.MESH
    barrier = pltpu.get_barrier_semaphore()
    for r in range(1, nk):
        pl.semaphore_signal(
            barrier, inc=1, device_id=(lax.rem(k + r, nk), j), device_id_type=mesh_id
        )
    for s in range(1, npart):
        pl.semaphore_signal(
            barrier, inc=1, device_id=(k, lax.rem(j + s, npart)), device_id_type=mesh_id
        )
    pl.semaphore_wait(barrier, nk + npart - 2)

    targets = ((v_ref, val_ref, k * npart + j), (c_ref, cond_ref, k), (t_ref, trial_ref, k))
    far = []
    for r in range(1, nk):
        row = []
        for i, (here, there, slot) in enumerate(targets):
            copy = pltpu.make_async_remote_copy(
                src_ref=here,
                dst_ref=there.at[slot],
                send_sem=far_send.at[i, r],
                recv_sem=far_recv.at[i, r],
                device_id=(lax.rem(k + r, nk), j),
                device_id_type=mesh_id,
            )
            copy.start()
            row.append(copy)
        far.append(row)
    own = []
    for i, (here, there, slot) in enumerate(targets):
        copy = pltpu.make_async_copy(here, there.at[slot], own_sem.at[i])
        copy.start()
        own.append(copy)

    near = []

    def pass_on(r, block, slot):
        for s in range(1, npart):
            copy = pltpu.make_async_remote_copy(
                src_ref=block,
                dst_ref=val_ref.at[slot],
                send_sem=near_send.at[r, s],
                recv_sem=near_recv.at[r, s],
                device_id=(k, lax.rem(j + s, npart)),
                device_id_type=mesh_id,
            )
            copy.start()
            near.append(copy)

    pass_on(0, v_ref, k * npart + j)
    for r in range(1, nk):
        far[r - 1][0].wait_recv()
        slot = lax.rem(k - r + nk, nk) * npart + j
        pass_on(r, val_ref.at[slot], slot)
    for row in far:
        for copy in row[1:]:
            copy.wait_recv()
    for copy in near:
        copy.wait_recv()
    for copy in own:
        copy.wait()
    for row in far:
        for copy in row:
            copy.wait_send()
    for copy in near:
        copy.wait_send()


def gather_all(valence, conduction, turned, nk, npart):
    bands, width = valence.shape
    if nk * npart > 64:
        return (
            lax.all_gather(valence, ("ka", "pts"), axis=0),
            lax.all_gather(conduction, "ka", axis=0),
            lax.all_gather(turned, "ka", axis=0),
        )
    vm = pl.BlockSpec(memory_space=pltpu.VMEM)
    return pl.pallas_call(
        functools.partial(gather_kernel, nk, npart),
        out_shape=(
            jax.ShapeDtypeStruct((nk * npart,) + valence.shape, valence.dtype),
            jax.ShapeDtypeStruct((nk,) + conduction.shape, conduction.dtype),
            jax.ShapeDtypeStruct((nk,) + turned.shape, turned.dtype),
        ),
        in_specs=[vm] * 3,
        out_specs=(vm,) * 3,
        scratch_shapes=[
            pltpu.SemaphoreType.DMA((3, nk)),
            pltpu.SemaphoreType.DMA((3, nk)),
            pltpu.SemaphoreType.DMA((nk, npart)),
            pltpu.SemaphoreType.DMA((nk, npart)),
            pltpu.SemaphoreType.DMA((3,)),
        ],
        compiler_params=pltpu.CompilerParams(
            collective_id=0, has_side_effects=True, vmem_limit_bytes=16 * 1024 * 1024
        ),
    )(valence, conduction, turned)


def reduce_kernel(nk, npart, part_ref, out_ref, held, send_sem, recv_sem):
    count = nk * npart
    me = lax.axis_index("ka") * npart + lax.axis_index("pts")
    mesh_id = pl.DeviceIdType.MESH
    barrier = pltpu.get_barrier_semaphore()

    def device(r):
        to = lax.rem(me + r, count)
        return to, (to // npart, lax.rem(to, npart))

    def greet(r, c):
        pl.semaphore_signal(barrier, inc=1, device_id=device(r)[1], device_id_type=mesh_id)
        return c

    lax.fori_loop(1, count, greet, 0)
    pl.semaphore_wait(barrier, count - 1)

    def copy_of(r):
        to, where = device(r)
        return pltpu.make_async_remote_copy(
            src_ref=part_ref.at[to],
            dst_ref=held.at[r],
            send_sem=send_sem.at[r],
            recv_sem=recv_sem.at[r],
            device_id=where,
            device_id_type=mesh_id,
        )

    def send(r, c):
        copy_of(r).start()
        return c

    lax.fori_loop(1, count, send, 0)
    out_ref[...] = part_ref[me]

    def take(r, c):
        copy_of(r).wait_recv()
        out_ref[...] += held[r]
        return c

    lax.fori_loop(1, count, take, 0)

    def finish(r, c):
        copy_of(r).wait_send()
        return c

    lax.fori_loop(1, count, finish, 0)


def reduce_all(part, nk, npart):
    count = nk * npart
    if count > 64:
        return lax.psum_scatter(part, ("ka", "pts"), scatter_dimension=0, tiled=True)
    vm = pl.BlockSpec(memory_space=pltpu.VMEM)
    return pl.pallas_call(
        functools.partial(reduce_kernel, nk, npart),
        out_shape=jax.ShapeDtypeStruct(part.shape[1:], part.dtype),
        in_specs=[vm],
        out_specs=vm,
        scratch_shapes=[
            pltpu.VMEM(part.shape, part.dtype),
            pltpu.SemaphoreType.DMA((count,)),
            pltpu.SemaphoreType.DMA((count,)),
        ],
        compiler_params=pltpu.CompilerParams(collective_id=1, has_side_effects=True),
    )(part)


def panel_kernel(
    active, partner, w_ref, val_ref, cond_ref, trial_ref, out_ref,
    pair_a, pair_b, z_a, z_b, block_a, block_b, back_ref,
    *, nk, npart, bands, ntrial, rows,
):
    width = val_ref.shape[2]
    points = w_ref.shape[0]
    steps = points // rows
    each = npart // steps
    pairs, zs, blocks = (pair_a, pair_b), (z_a, z_b), (block_a, block_b)
    out_ref[...] = jnp.zeros_like(out_ref)

    def build(k, to, j):
        own = val_ref[k * npart + j]
        far = val_ref[partner[k] * npart + j]
        cols = pl.ds(j * width, width)
        for v in range(bands):
            to[v * bands : (v + 1) * bands, cols] = own * far[v : v + 1, :]

    def sum_bands(z_ref, block_ref, k, b):
        for l in range(rows // 128):
            here = slice(l * 128, (l + 1) * 128)
            mine = slice(b * rows + l * 128, b * rows + (l + 1) * 128)
            acc = [jnp.zeros((bands, 128), jnp.float32) for _ in range(ntrial)]
            for v in range(bands):
                z = z_ref[v * bands : (v + 1) * bands, here]
                for t in range(ntrial):
                    acc[t] = acc[t] + z * block_ref[t * bands + v : t * bands + v + 1, mine]
            for t in range(ntrial):
                back_ref[t * bands : (t + 1) * bands, here] = acc[t]
        back = back_ref[...]
        high = back.astype(jnp.bfloat16)
        low = (back - high.astype(jnp.float32)).astype(jnp.bfloat16)
        cond = cond_ref[k, :, b * rows : (b + 1) * rows]
        out_ref[k] += dot_nt(cond, high) + dot_nt(cond, low)

    def two(i, carry):
        for half in range(2):
            k = 2 * i + half
            before = lax.rem(k + nk - 1, nk)
            after = lax.rem(k + 1, nk)
            for b in range(steps):
                turn = half * steps + b
                zs[turn % 2][...] = dot_nt(pairs[half][...], w_ref[b * rows : (b + 1) * rows, :])
                for j in range(b * each, (b + 1) * each):
                    build(after, pairs[1 - half], j)
                if b == 0:
                    sum_bands(zs[(turn + 1) % 2], blocks[1 - half], before, steps - 1)
                    p = partner[k]
                    blocks[half][...] = (
                        lax.dot_general(
                            trial_ref[p], cond_ref[p], TN, preferred_element_type=jnp.float32
                        )
                        .astype(jnp.bfloat16)
                        .astype(jnp.float32)
                    )
                else:
                    sum_bands(zs[(turn + 1) % 2], blocks[half], k, b - 1)
        return carry

    @pl.when(active[0] > 0)
    def _():
        z_b[...] = jnp.zeros_like(z_b)
        block_b[...] = jnp.zeros_like(block_b)
        for j in range(npart):
            build(0, pair_a, j)
        lax.fori_loop(0, nk // 2, two, 0)
        sum_bands(z_b, block_b, nk - 1, steps - 1)


def panel_term(active, partner, w, val, cond, trial, npart, ntrial):
    nk, conds, _ = cond.shape
    bands = val.shape[1]
    points, total = w.shape
    rows = min(256, points)
    vm = pl.BlockSpec(memory_space=pltpu.VMEM)
    sm = pl.BlockSpec(memory_space=pltpu.SMEM)
    pair = pltpu.VMEM((bands * bands, total), jnp.bfloat16)
    z = pltpu.VMEM((bands * bands, rows), jnp.float32)
    block = pltpu.VMEM((ntrial * bands, points), jnp.float32)
    return pl.pallas_call(
        functools.partial(
            panel_kernel, nk=nk, npart=npart, bands=bands, ntrial=ntrial, rows=rows
        ),
        out_shape=jax.ShapeDtypeStruct((nk, conds, ntrial * bands), jnp.float32),
        in_specs=[sm, sm, vm, vm, vm, vm],
        out_specs=vm,
        scratch_shapes=[
            pair, pair, z, z, block, block,
            pltpu.VMEM((ntrial * bands, rows), jnp.float32),
        ],
        compiler_params=pltpu.CompilerParams(vmem_limit_bytes=50 * 1024 * 1024),
    )(active, partner, w, val, cond, trial)


def shards(valence, conduction, trials, w_panels, partner, owner):
    nk = lax.axis_size("ka")
    npart = lax.axis_size("pts")
    me = lax.axis_index("ka")
    bands = valence.shape[1]
    conds = conduction.shape[1]
    ntrial = trials.shape[2] // conds
    turned = trials[0].reshape(bands, conds, ntrial).transpose(1, 2, 0)
    turned = turned.reshape(conds, ntrial * bands)
    val, cond, trial = gather_all(valence[0], conduction[0], turned, nk, npart)
    hit = owner == me
    active = jnp.any(hit).astype(jnp.int32).reshape(1)
    mine = jnp.sum(jnp.where(hit[:, None], partner, 0), axis=0).astype(jnp.int32)
    part = panel_term(active, mine, w_panels[0], val, cond, trial, npart, ntrial)
    share = conds // npart
    total = reduce_all(part.reshape(nk * npart, share, ntrial * bands), nk, npart)
    return (
        total.reshape(share, ntrial, bands).transpose(2, 0, 1).reshape(1, bands, share * ntrial)
    )


def solution(mesh):
    placed = (
        P("ka", None, "pts"),
        P("ka", None, "pts"),
        P("ka", None, None),
        P("ka", "pts", None),
        P(),
        P(),
    )
    return jax.shard_map(
        shards, mesh=mesh, in_specs=placed, out_specs=P("ka", None, "pts"), check_vma=False
    )
```
